32 devices in a mesh: scene: 2 (over y), az: 8 (over z, x), rg: 2 (over core).
Axes of the slice: x: 2, y: 2, z: 4, core: 2. Of those that a mesh axis runs over, the one named last changes fastest.
Arguments:
- raw_echo: bfloat16 [2, 1024, 4480], P(None, ('scene', 'az'), 'rg'), parts along dimension 1, may hold values from -6 to 6
- chirp: bfloat16 [2, 4096], replicated, may hold values from -0.09375 to 0.09375
- interp_weight: bfloat16 [8, 128], P(None, 'rg'), may hold values from -2 to 2
- band_shift: int32 [128], P('rg'), may hold values from 0 to 248
- doppler_bin: int32 [256], P('scene'), parts along dimension 0, may hold values from -64 to 64
Outputs:
- focused: float32 [256, 2, 512], P(('scene', 'rg', 'az')), parts along dimension 0
The draws below stay inside these ranges and needn't reach their ends.
There are 2 independent parts, one for each index of `scene`. The reference program is written for one: setup_inputs(seed, part) draws one part's arguments, and reference() takes and returns one part's arrays. A program takes and returns all parts, laid end to end along the dimension named above; an argument that names none is the same for every part. Nothing has to cross between parts.
All inputs are finite; a program needn't handle non-finite values.
Results may differ from the reference program's by a relative error of at most 0.0051.
Values may be sent and summed in bfloat16 or wider, within the bound.
A program may use at most 128 MiB of HBM per device.

```python
import math
import jax
import jax.numpy as jnp
from jax import lax

RANGE_TAPS = 4096
AZ_TAPS = 2048
BAND = 8
MIGR = 256
A_DEV = 64
RBIN_DEV = 8
NR = 128
NA = 512
RAWLEN = 4480
N_AZ = 8


def place_ends(array, rng, least, top_value):
    place = [jax.random.randint(jax.random.fold_in(rng, axis), (), 0, length) for axis, length in enumerate(array.shape)]
    main_axis = array.shape.index(max(array.shape))
    neighbour = place[:main_axis] + [(place[main_axis] + 1) % array.shape[main_axis]] + place[main_axis + 1:]
    return array.at[tuple(place)].set(least).at[tuple(neighbour)].set(top_value)


def shard_levels(key, shape, split, smallest, high):
    loudness = 1.0
    for axis_at, shards_of in split:
        steps = jax.random.uniform(jax.random.fold_in(jax.random.fold_in(key, 6), axis_at), (shards_of,), jnp.float32, smallest / len(split), high / len(split))
        loudness = loudness * jnp.repeat(jnp.exp(steps), shape[axis_at] // shards_of).reshape((-1,) + (1,) * (len(shape) - 1 - axis_at))
    return loudness


def noise(own_key, extent, deviation, bound, split=(), kind=jnp.bfloat16):
    drawn = jax.random.normal(own_key, extent, jnp.float32) * deviation
    if len(split) > 0:
        drawn = shard_levels(own_key, extent, split, -0.22, 0.18) * drawn
    return jnp.clip(drawn, min=-bound, max=bound).astype(kind)


def setup_inputs(seed: int = 0, part: int = 0) -> dict:
    splits = jax.random.split(jax.random.key(seed), 6)
    part_splits = jax.random.split(jax.random.fold_in(splits[5], part), 6)
    raw_echo = noise(part_splits[0], (2, NA, RAWLEN), 1.0, 6.0, ((1, 8), (2, 2)))
    chirp = noise(splits[1], (2, RANGE_TAPS), RANGE_TAPS ** -0.5, 0.09375)
    interp_weight = noise(splits[2], (BAND, NR), BAND ** -0.5, 2.0, ((1, 2),))
    band_shift = place_ends(jax.random.randint(splits[3], (NR,), 0, MIGR - BAND + 1), jax.random.fold_in(splits[3], 1), 0, MIGR - BAND).astype(jnp.int32)
    doppler_bin = place_ends(jax.random.randint(part_splits[4], (NR,), -(AZ_TAPS // 32), AZ_TAPS // 32 + 1), jax.random.fold_in(part_splits[4], 1), -(AZ_TAPS // 32), (AZ_TAPS // 32 + 1) - 1).astype(jnp.int32)
    return {"raw_echo": raw_echo, "chirp": chirp, "interp_weight": interp_weight, "band_shift": band_shift, "doppler_bin": doppler_bin}


def filter_taps(offset, beta, doppler):
    centered = offset - 0.5 * AZ_TAPS
    phase = math.pi * beta * (centered * centered) / AZ_TAPS + 2.0 * math.pi / AZ_TAPS * doppler * centered
    amplitude = (0.54 - 0.46 * jnp.cos(2.0 * math.pi / (AZ_TAPS - 1) * offset)) / math.sqrt(0.4 * AZ_TAPS)
    return (amplitude * jnp.cos(phase), amplitude * jnp.sin(phase))

def reference(raw_echo, chirp, interp_weight, band_shift, doppler_bin):
    raw = raw_echo.astype(jnp.float32)
    replica = chirp.astype(jnp.float32)
    ext_total = NR + MIGR
    range_fft = 1 << (RAWLEN + RANGE_TAPS).bit_length()
    replica_spec = jnp.fft.fft(replica[0] + 1j * replica[1], range_fft)
    band_index = (jnp.arange(NR, dtype=jnp.int32)[:, None] + band_shift[:, None] + jnp.arange(BAND, dtype=jnp.int32)[None, :]).astype(jnp.int32)
    weights = interp_weight.astype(jnp.float32).T

    def line_block(block):
        spectrum = jnp.fft.fft(block[0] + 1j * block[1], range_fft, axis=-1)
        correl = jnp.fft.ifft(spectrum * jnp.conj(replica_spec)[None, :], axis=-1)[:, :ext_total]
        parts = []
        for piece in (jnp.real(correl), jnp.imag(correl)):
            rounded = piece.astype(jnp.bfloat16).astype(jnp.float32)
            picked = rounded[:, band_index]
            parts.append(lax.optimization_barrier(jnp.sum(picked * weights[None, :, :], axis=-1)).astype(jnp.bfloat16))
        return jnp.stack(parts, axis=0)
    blocks = raw.reshape(2, N_AZ, A_DEV, RAWLEN).transpose(1, 0, 2, 3)
    migrated = lax.map(line_block, blocks)
    migrated = migrated.transpose(3, 1, 0, 2).reshape(NR, 2, NA)
    offsets = jnp.arange(AZ_TAPS, dtype=jnp.int32).astype(jnp.float32)
    bins = jnp.arange(NR, dtype=jnp.int32).astype(jnp.float32)
    beta = 0.5 + 0.5 * bins / NR
    tap_re, tap_im = filter_taps(offsets[None, :], beta[:, None], doppler_bin.astype(jnp.float32)[:, None])
    tap_re = tap_re.astype(jnp.bfloat16).astype(jnp.float32)
    tap_im = tap_im.astype(jnp.bfloat16).astype(jnp.float32)
    az_fft = 1 << (NA + 2 * AZ_TAPS).bit_length()

    def bin_block(args):
        lines, hre, him = args
        signal = lines[:, 0].astype(jnp.float32) + 1j * lines[:, 1].astype(jnp.float32)
        signal = jnp.pad(signal, ((0, 0), (AZ_TAPS // 2, 0)))
        spectrum = jnp.fft.fft(signal, az_fft, axis=-1)
        conj_taps = jnp.fft.fft(hre - 1j * him, az_fft, axis=-1)
        result = jnp.fft.ifft(spectrum * jnp.conj(conj_taps), axis=-1)[:, :NA]
        return jnp.stack([jnp.real(result), jnp.imag(result)], axis=1).astype(jnp.float32)
    count = NR // RBIN_DEV
    focused = lax.map(bin_block, (migrated.reshape(count, RBIN_DEV, 2, NA), tap_re.reshape(count, RBIN_DEV, AZ_TAPS), tap_im.reshape(count, RBIN_DEV, AZ_TAPS)))
    return focused.reshape(NR, 2, NA)
```

```python
import functools
import math

import jax
import jax.numpy as jnp
from jax import lax
from jax.experimental import pallas as pl
from jax.experimental.pallas import tpu as pltpu
from jax.sharding import PartitionSpec as P

AZ_TAPS = 2048
AZ_TILE = 128
TILE = 128
MESH = pl.DeviceIdType.MESH


def partner(value, axis, bit):
    return lax.ppermute(value, axis, [(i, i ^ 1 << bit) for i in range(lax.axis_size(axis))])


def filter_taps(offset, beta, doppler):
    centered = offset - 0.5 * AZ_TAPS
    phase = (
        math.pi * beta * (centered * centered) / AZ_TAPS
        + 2.0 * math.pi / AZ_TAPS * doppler * centered
    )
    amplitude = (0.54 - 0.46 * jnp.cos(2.0 * math.pi / (AZ_TAPS - 1) * offset)) / math.sqrt(
        0.4 * AZ_TAPS
    )
    return (amplitude * jnp.cos(phase), amplitude * jnp.sin(phase))


def shifted_rows(vector, rows):
    taps = vector.shape[0]
    padded = jnp.concatenate([vector, jnp.zeros((rows + 1,), vector.dtype)])
    repeated = jnp.tile(padded, rows)[: rows * (taps + rows)]
    return repeated.reshape(rows, taps + rows)


def range_and_migration(window, kernel, mig_matrix, tile, extent):
    lines = window.shape[1]
    width = kernel.shape[1] // 2
    count = extent // tile
    starts = jnp.arange(count, dtype=jnp.int32) * tile

    def tile_window(start):
        piece = lax.dynamic_slice_in_dim(window, start, width, 2)
        return jnp.concatenate([piece[0], piece[1]], axis=1)

    stacked = jax.vmap(tile_window)(starts).reshape(count * lines, 2 * width)
    tiles_out = lax.dot_general(
        stacked, kernel, (((1,), (1,)), ((), ())), preferred_element_type=jnp.float32
    )
    range_lines = (
        tiles_out.reshape(count, lines, 2, tile).transpose(2, 1, 0, 3).reshape(2 * lines, extent)
    )
    range_lines = range_lines.astype(jnp.bfloat16)
    moved = lax.dot_general(
        mig_matrix, range_lines, (((0,), (1,)), ((), ())), preferred_element_type=jnp.float32
    )
    return moved.astype(jnp.bfloat16).reshape(mig_matrix.shape[1], 2, lines)


def per_device(raw_echo, chirp, interp_weight, band_shift, doppler_bin):
    rg_index = lax.axis_index("rg")
    az_index = lax.axis_index("az")
    half_len = raw_echo.shape[2]
    taps = chirp.shape[1]
    bands = interp_weight.shape[0]
    slab = interp_weight.shape[1]
    extent = 2 * half_len - slab - taps
    tile = min(128, slab)
    margin_len = half_len - slab
    outgoing = lax.dynamic_slice_in_dim(raw_echo, (1 - rg_index) * slab, margin_len, 2)
    incoming = partner(outgoing, "rg", 0)
    window = jnp.where(
        rg_index == 0,
        jnp.concatenate([raw_echo, incoming], axis=2),
        jnp.concatenate([incoming, raw_echo], axis=2),
    )
    rows_re = shifted_rows(chirp[0], tile)
    rows_im = shifted_rows(chirp[1], tile)
    kernel = jnp.concatenate(
        [jnp.concatenate([rows_re, rows_im], axis=1), jnp.concatenate([-rows_im, rows_re], axis=1)],
        axis=0,
    )
    position = lax.broadcasted_iota(jnp.int32, (extent, slab), 0)
    column = lax.broadcasted_iota(jnp.int32, (extent, slab), 1)
    offset = position - column - band_shift[None, :]
    mig_matrix = jnp.zeros((extent, slab), jnp.bfloat16)
    for tap in range(bands):
        mig_matrix = mig_matrix + jnp.where(
            offset == tap, interp_weight[tap][None, :], jnp.zeros((), jnp.bfloat16)
        )
    migrated = range_and_migration(window, kernel, mig_matrix, tile, extent)
    turned = lax.all_to_all(migrated, "az", split_axis=0, concat_axis=2, tiled=True)
    bins_here = turned.shape[0]
    total_lines = turned.shape[2]
    total_bins = slab * lax.axis_size("rg")
    first_bin = rg_index * slab + az_index * bins_here
    doppler = lax.dynamic_slice_in_dim(doppler_bin, first_bin, bins_here).astype(jnp.float32)
    global_bins = (first_bin + jnp.arange(bins_here, dtype=jnp.int32)).astype(jnp.float32)
    beta = 0.5 + 0.5 * global_bins / total_bins
    span = AZ_TAPS // AZ_TILE + 1
    tile_count = total_lines // AZ_TILE
    block_count = (total_lines + AZ_TAPS) // AZ_TILE
    out_index = lax.broadcasted_iota(jnp.int32, (AZ_TILE, AZ_TILE + AZ_TAPS), 0)
    in_index = lax.broadcasted_iota(jnp.int32, (AZ_TILE, AZ_TILE + AZ_TAPS), 1)
    lag = in_index - out_index
    inside = (lag >= 0) & (lag < AZ_TAPS)
    lag_float = lag.astype(jnp.float32)

    def one_bin(args):
        signal, shift, rate = args
        padded = jnp.pad(signal, ((0, 0), (AZ_TAPS // 2, AZ_TAPS // 2)))
        blocks = padded.reshape(2, block_count, AZ_TILE)
        windows = jnp.concatenate(
            [blocks[:, start : start + tile_count] for start in range(span)], axis=2
        )
        left = jnp.concatenate([windows[0], windows[1]], axis=1)
        value_re, value_im = filter_taps(lag_float, rate, shift)
        value_re = jnp.where(inside, value_re, 0.0).astype(jnp.bfloat16)
        value_im = jnp.where(inside, value_im, 0.0).astype(jnp.bfloat16)
        az_kernel = jnp.concatenate(
            [
                jnp.concatenate([value_re, -value_im], axis=1),
                jnp.concatenate([value_im, value_re], axis=1),
            ],
            axis=0,
        )
        result = lax.dot_general(
            left, az_kernel, (((1,), (1,)), ((), ())), preferred_element_type=jnp.float32
        )
        return result.reshape(tile_count, 2, AZ_TILE).transpose(1, 0, 2).reshape(2, total_lines)

    return lax.map(one_bin, (turned, doppler, beta))


def toeplitz_rows(row, rows):
    return pltpu.roll(jnp.broadcast_to(row, (rows, row.shape[1])), 0, 1, stride=1, stride_axis=0)


def column(row, first, rows):
    width = row.shape[1]
    lane = lax.broadcasted_iota(jnp.int32, (rows, width), 1)
    sub = lax.broadcasted_iota(jnp.int32, (rows, width), 0)
    picked = jnp.where(lane == sub + first, jnp.broadcast_to(row, (rows, width)), 0.0)
    return jnp.sum(picked, axis=1, keepdims=True)


def dot_nt(left, right):
    return lax.dot_general(
        left, right, (((1,), (1,)), ((), ())), preferred_element_type=jnp.float32
    )


def fused_kernel(
    azs, raw, chirp, weight, shift, doppler, out,
    halves, full, chirp_rows, az_rows, moved, slots, spread,
    local_sem, pair_send, pair_recv, turn_send, turn_recv,
):
    az = lax.axis_index("az")
    rg = lax.axis_index("rg")
    lines = raw.shape[1]
    slab = weight.shape[1]
    bins = out.shape[0]
    tiles_az = out.shape[2]
    taps = chirp.shape[1]
    width = taps + TILE
    extent = full.shape[1] - taps

    barrier = pltpu.get_barrier_semaphore()
    pl.semaphore_signal(barrier, inc=1, device_id={"rg": 1 - rg}, device_id_type=MESH)
    for step in range(1, azs):
        pl.semaphore_signal(
            barrier, inc=1, device_id={"az": lax.rem(az + step, azs)}, device_id_type=MESH
        )
    own = pltpu.make_async_copy(raw, halves.at[rg], local_sem)
    own.start()
    pl.semaphore_wait(barrier, azs)
    pair = pltpu.make_async_remote_copy(
        src_ref=raw, dst_ref=halves.at[rg], send_sem=pair_send, recv_sem=pair_recv,
        device_id={"rg": 1 - rg}, device_id_type=MESH,
    )
    pair.start()

    for part in range(2):
        padded = jnp.concatenate(
            [chirp[part : part + 1, :].astype(jnp.float32), jnp.zeros((1, TILE), jnp.float32)],
            axis=1,
        )
        chirp_rows[part * TILE : (part + 1) * TILE, :] = toeplitz_rows(padded, TILE).astype(
            jnp.bfloat16
        )

    span = (2 * tiles_az - 1) * TILE
    wheel = span + TILE
    first_bin = rg * slab + az * bins
    place = lax.broadcasted_iota(jnp.int32, (bins, wheel), 1)
    lag = place + AZ_TAPS // 2 - (tiles_az - 1) * TILE - jnp.where(place >= span, wheel, 0)
    bin_index = first_bin + lax.broadcasted_iota(jnp.int32, (bins, wheel), 0)
    beta = 0.5 + 0.5 * bin_index.astype(jnp.float32) / (2 * slab)
    rate = column(doppler[...].astype(jnp.float32), first_bin, bins)
    value_re, value_im = filter_taps(lag.astype(jnp.float32), beta, rate)
    for part, value in enumerate((value_re, value_im)):
        value = value.astype(jnp.bfloat16).astype(jnp.float32)
        for b in range(bins):
            rows = toeplitz_rows(value[b : b + 1, :], TILE)
            az_rows[b, part * TILE : (part + 1) * TILE, :] = rows[:, :span].astype(jnp.bfloat16)

    position = lax.broadcasted_iota(jnp.int32, (slab, extent), 1)
    bin_at = lax.broadcasted_iota(jnp.int32, (slab, extent), 0) + rg * slab
    start = column(shift[...].astype(jnp.float32), 0, slab).astype(jnp.int32)
    offset = position - bin_at - start
    mig = jnp.zeros((slab, extent), jnp.float32)
    for tap in range(weight.shape[0]):
        tap_weight = column(weight[tap : tap + 1, :].astype(jnp.float32), 0, slab)
        mig = jnp.where(offset == tap, tap_weight, mig)
    mig = mig.astype(jnp.bfloat16)

    own.wait()
    pair.wait()
    half_len = raw.shape[2]
    full[...] = jnp.concatenate(
        [halves[0].reshape(2 * lines, half_len), halves[1].reshape(2 * lines, half_len)], axis=1
    )
    kernel = chirp_rows[...]
    pieces = []
    for t in range(extent // TILE):
        product = dot_nt(full[:, t * TILE : t * TILE + width], kernel)
        real = product[:lines, :TILE] + product[lines:, TILE:]
        imag = product[lines:, :TILE] - product[:lines, TILE:]
        pieces.append(jnp.concatenate([real, imag], axis=0).astype(jnp.bfloat16))
    range_lines = jnp.concatenate(pieces, axis=1)
    moved[...] = dot_nt(mig, range_lines).astype(jnp.bfloat16).astype(jnp.float32)

    def block(index):
        return moved.at[pl.ds(pl.multiple_of(index * bins, bins), bins), :]

    copies = []
    for step in range(1, azs):
        peer = lax.rem(az + step, azs)
        copy = pltpu.make_async_remote_copy(
            src_ref=block(peer), dst_ref=slots.at[az], send_sem=turn_send.at[step],
            recv_sem=turn_recv.at[az], device_id={"az": peer}, device_id_type=MESH,
        )
        copy.start()
        copies.append(copy)
    slots[az] = block(az)[...]
    for step in range(1, azs):
        peer = lax.rem(az + step, azs)
        pltpu.make_async_remote_copy(
            src_ref=block(peer), dst_ref=slots.at[peer], send_sem=turn_send.at[step],
            recv_sem=turn_recv.at[peer], device_id={"az": peer}, device_id_type=MESH,
        ).wait_recv()

    apron = jnp.zeros((bins, (tiles_az - 1) * TILE), jnp.float32)
    for part in range(2):
        signal = jnp.concatenate(
            [slots[i][:, part * lines : (part + 1) * lines] for i in range(azs)], axis=1
        )
        signal = jnp.concatenate([apron, signal, apron], axis=1)
        for t in range(tiles_az):
            spread[part * tiles_az + t] = signal[:, t * TILE : t * TILE + span]
    for b in range(bins):
        product = dot_nt(spread[:, b, :].astype(jnp.bfloat16), az_rows[b])
        out[b, 0] = product[:tiles_az, :TILE] - product[tiles_az:, TILE:]
        out[b, 1] = product[tiles_az:, :TILE] + product[:tiles_az, TILE:]
    for copy in copies:
        copy.wait_send()


def fused(raw_echo, chirp, interp_weight, band_shift, doppler_bin):
    azs = lax.axis_size("az")
    lines, half_len = raw_echo.shape[1:]
    taps = chirp.shape[1]
    slab = interp_weight.shape[1]
    bins = slab // azs
    tiles_az = azs * lines // TILE
    span = (2 * tiles_az - 1) * TILE
    vmem = pl.BlockSpec(memory_space=pltpu.VMEM)
    result = pl.pallas_call(
        functools.partial(fused_kernel, azs),
        out_shape=jax.ShapeDtypeStruct((bins, 2, tiles_az, TILE), jnp.float32),
        in_specs=[pl.BlockSpec(memory_space=pl.ANY), vmem, vmem, vmem, vmem],
        out_specs=vmem,
        scratch_shapes=[
            pltpu.VMEM((2, 2, lines, half_len), jnp.bfloat16),
            pltpu.VMEM((2 * lines, 2 * half_len), jnp.bfloat16),
            pltpu.VMEM((2 * TILE, taps + TILE), jnp.bfloat16),
            pltpu.VMEM((bins, 2 * TILE, span), jnp.bfloat16),
            pltpu.VMEM((slab, 2 * lines), jnp.float32),
            pltpu.VMEM((azs, bins, 2 * lines), jnp.float32),
            pltpu.VMEM((2 * tiles_az, bins, span), jnp.float32),
            pltpu.SemaphoreType.DMA,
            pltpu.SemaphoreType.DMA,
            pltpu.SemaphoreType.DMA,
            pltpu.SemaphoreType.DMA((azs,)),
            pltpu.SemaphoreType.DMA((azs,)),
        ],
        compiler_params=pltpu.CompilerParams(
            collective_id=0, has_side_effects=True, vmem_limit_bytes=48 * 1024 * 1024
        ),
    )(raw_echo, chirp, interp_weight, band_shift.reshape(1, -1), doppler_bin.reshape(1, -1))
    return result.reshape(bins, 2, tiles_az * TILE)


def local(raw_echo, chirp, interp_weight, band_shift, doppler_bin):
    azs = lax.axis_size("az")
    lines, half_len = raw_echo.shape[1:]
    total_lines = azs * lines
    extent = 2 * half_len - chirp.shape[1]
    small = (
        lax.axis_size("rg") == 2
        and interp_weight.shape[1] == 8 * azs
        and 2 * lines == TILE
        and total_lines % TILE == 0
        and total_lines <= AZ_TAPS // 4
        and extent % TILE == 0
        and extent <= 512
    )
    run = fused if small else per_device
    return run(raw_echo, chirp, interp_weight, band_shift, doppler_bin)


def solution(mesh):
    placed = (P(None, ("scene", "az"), "rg"), P(), P(None, "rg"), P("rg"), P("scene"))
    return jax.shard_map(
        local,
        mesh=mesh,
        in_specs=placed,
        out_specs=P(("scene", "rg", "az"), None, None),
        check_vma=False,
    )
```

```python
import functools
import math

import jax
import jax.numpy as jnp
from jax import lax
from jax.experimental import pallas as pl
from jax.experimental.pallas import tpu as pltpu
from jax.sharding import PartitionSpec as P

AZ_TAPS = 2048
AZ_TILE = 128
TILE = 128
MESH = pl.DeviceIdType.MESH


def partner(value, axis, bit):
    return lax.ppermute(value, axis, [(i, i ^ 1 << bit) for i in range(lax.axis_size(axis))])


def filter_taps(offset, beta, doppler):
    centered = offset - 0.5 * AZ_TAPS
    phase = (
        math.pi * beta * (centered * centered) / AZ_TAPS
        + 2.0 * math.pi / AZ_TAPS * doppler * centered
    )
    amplitude = (0.54 - 0.46 * jnp.cos(2.0 * math.pi / (AZ_TAPS - 1) * offset)) / math.sqrt(
        0.4 * AZ_TAPS
    )
    return (amplitude * jnp.cos(phase), amplitude * jnp.sin(phase))


def shifted_rows(vector, rows):
    taps = vector.shape[0]
    padded = jnp.concatenate([vector, jnp.zeros((rows + 1,), vector.dtype)])
    repeated = jnp.tile(padded, rows)[: rows * (taps + rows)]
    return repeated.reshape(rows, taps + rows)


def range_and_migration(window, kernel, mig_matrix, tile, extent):
    lines = window.shape[1]
    width = kernel.shape[1] // 2
    count = extent // tile
    starts = jnp.arange(count, dtype=jnp.int32) * tile

    def tile_window(start):
        piece = lax.dynamic_slice_in_dim(window, start, width, 2)
        return jnp.concatenate([piece[0], piece[1]], axis=1)

    stacked = jax.vmap(tile_window)(starts).reshape(count * lines, 2 * width)
    tiles_out = lax.dot_general(
        stacked, kernel, (((1,), (1,)), ((), ())), preferred_element_type=jnp.float32
    )
    range_lines = (
        tiles_out.reshape(count, lines, 2, tile).transpose(2, 1, 0, 3).reshape(2 * lines, extent)
    )
    range_lines = range_lines.astype(jnp.bfloat16)
    moved = lax.dot_general(
        mig_matrix, range_lines, (((0,), (1,)), ((), ())), preferred_element_type=jnp.float32
    )
    return moved.astype(jnp.bfloat16).reshape(mig_matrix.shape[1], 2, lines)


def per_device(raw_echo, chirp, interp_weight, band_shift, doppler_bin):
    rg_index = lax.axis_index("rg")
    az_index = lax.axis_index("az")
    half_len = raw_echo.shape[2]
    taps = chirp.shape[1]
    bands = interp_weight.shape[0]
    slab = interp_weight.shape[1]
    extent = 2 * half_len - slab - taps
    tile = min(128, slab)
    margin_len = half_len - slab
    outgoing = lax.dynamic_slice_in_dim(raw_echo, (1 - rg_index) * slab, margin_len, 2)
    incoming = partner(outgoing, "rg", 0)
    window = jnp.where(
        rg_index == 0,
        jnp.concatenate([raw_echo, incoming], axis=2),
        jnp.concatenate([incoming, raw_echo], axis=2),
    )
    rows_re = shifted_rows(chirp[0], tile)
    rows_im = shifted_rows(chirp[1], tile)
    kernel = jnp.concatenate(
        [jnp.concatenate([rows_re, rows_im], axis=1), jnp.concatenate([-rows_im, rows_re], axis=1)],
        axis=0,
    )
    position = lax.broadcasted_iota(jnp.int32, (extent, slab), 0)
    column = lax.broadcasted_iota(jnp.int32, (extent, slab), 1)
    offset = position - column - band_shift[None, :]
    mig_matrix = jnp.zeros((extent, slab), jnp.bfloat16)
    for tap in range(bands):
        mig_matrix = mig_matrix + jnp.where(
            offset == tap, interp_weight[tap][None, :], jnp.zeros((), jnp.bfloat16)
        )
    migrated = range_and_migration(window, kernel, mig_matrix, tile, extent)
    turned = lax.all_to_all(migrated, "az", split_axis=0, concat_axis=2, tiled=True)
    bins_here = turned.shape[0]
    total_lines = turned.shape[2]
    total_bins = slab * lax.axis_size("rg")
    first_bin = rg_index * slab + az_index * bins_here
    doppler = lax.dynamic_slice_in_dim(doppler_bin, first_bin, bins_here).astype(jnp.float32)
    global_bins = (first_bin + jnp.arange(bins_here, dtype=jnp.int32)).astype(jnp.float32)
    beta = 0.5 + 0.5 * global_bins / total_bins
    span = AZ_TAPS // AZ_TILE + 1
    tile_count = total_lines // AZ_TILE
    block_count = (total_lines + AZ_TAPS) // AZ_TILE
    out_index = lax.broadcasted_iota(jnp.int32, (AZ_TILE, AZ_TILE + AZ_TAPS), 0)
    in_index = lax.broadcasted_iota(jnp.int32, (AZ_TILE, AZ_TILE + AZ_TAPS), 1)
    lag = in_index - out_index
    inside = (lag >= 0) & (lag < AZ_TAPS)
    lag_float = lag.astype(jnp.float32)

    def one_bin(args):
        signal, shift, rate = args
        padded = jnp.pad(signal, ((0, 0), (AZ_TAPS // 2, AZ_TAPS // 2)))
        blocks = padded.reshape(2, block_count, AZ_TILE)
        windows = jnp.concatenate(
            [blocks[:, start : start + tile_count] for start in range(span)], axis=2
        )
        left = jnp.concatenate([windows[0], windows[1]], axis=1)
        value_re, value_im = filter_taps(lag_float, rate, shift)
        value_re = jnp.where(inside, value_re, 0.0).astype(jnp.bfloat16)
        value_im = jnp.where(inside, value_im, 0.0).astype(jnp.bfloat16)
        az_kernel = jnp.concatenate(
            [
                jnp.concatenate([value_re, -value_im], axis=1),
                jnp.concatenate([value_im, value_re], axis=1),
            ],
            axis=0,
        )
        result = lax.dot_general(
            left, az_kernel, (((1,), (1,)), ((), ())), preferred_element_type=jnp.float32
        )
        return result.reshape(tile_count, 2, AZ_TILE).transpose(1, 0, 2).reshape(2, total_lines)

    return lax.map(one_bin, (turned, doppler, beta))


def toeplitz_rows(row, rows):
    return pltpu.roll(jnp.broadcast_to(row, (rows, row.shape[1])), 0, 1, stride=1, stride_axis=0)


def column(row, first, rows):
    width = row.shape[1]
    lane = lax.broadcasted_iota(jnp.int32, (rows, width), 1)
    sub = lax.broadcasted_iota(jnp.int32, (rows, width), 0)
    picked = jnp.where(lane == sub + first, jnp.broadcast_to(row, (rows, width)), 0.0)
    return jnp.sum(picked, axis=1, keepdims=True)


def dot_nt(left, right):
    return lax.dot_general(
        left, right, (((1,), (1,)), ((), ())), preferred_element_type=jnp.float32
    )


def fused_kernel(
    azs, raw, chirp_in, weight_in, shift_in, doppler_in, out,
    chirp, weight, shift, doppler, small_sem, halves, full, chirp_rows, az_rows, moved, slots, spread, sums,
    local_sem, pair_send, pair_recv, turn_send, turn_recv,
):
    az = lax.axis_index("az")
    rg = lax.axis_index("rg")
    lines = raw.shape[1]
    slab = weight_in.shape[1]
    bins = out.shape[0]
    tiles_az = out.shape[2]
    taps = chirp.shape[1]
    width = taps + TILE
    extent = full.shape[1] - taps

    barrier = pltpu.get_barrier_semaphore()
    pl.semaphore_signal(barrier, inc=1, device_id={"rg": 1 - rg}, device_id_type=MESH)
    for step in range(1, azs):
        pl.semaphore_signal(
            barrier, inc=1, device_id={"az": lax.rem(az + step, azs)}, device_id_type=MESH
        )
    loads = [
        pltpu.make_async_copy(source, target, small_sem.at[i])
        for i, (source, target) in enumerate(
            ((chirp_in, chirp), (doppler_in, doppler), (shift_in, shift), (weight_in, weight))
        )
    ]
    for load in loads:
        load.start()
    own = pltpu.make_async_copy(raw, halves.at[rg], local_sem)
    own.start()
    pl.semaphore_wait(barrier, azs)
    pair = pltpu.make_async_remote_copy(
        src_ref=raw, dst_ref=halves.at[rg], send_sem=pair_send, recv_sem=pair_recv,
        device_id={"rg": 1 - rg}, device_id_type=MESH,
    )
    pair.start()

    for load in loads:
        load.wait()

    for part in range(2):
        padded = jnp.concatenate(
            [chirp[part : part + 1, :].astype(jnp.float32), jnp.zeros((1, TILE), jnp.float32)],
            axis=1,
        )
        chirp_rows[part * TILE : (part + 1) * TILE, :] = toeplitz_rows(padded, TILE).astype(
            jnp.bfloat16
        )

    span = (2 * tiles_az - 1) * TILE
    wheel = span + TILE
    first_bin = rg * slab + az * bins
    place = lax.broadcasted_iota(jnp.int32, (bins, wheel), 1)
    lag = place + AZ_TAPS // 2 - (tiles_az - 1) * TILE - jnp.where(place >= span, wheel, 0)
    bin_index = first_bin + lax.broadcasted_iota(jnp.int32, (bins, wheel), 0)
    beta = 0.5 + 0.5 * bin_index.astype(jnp.float32) / (2 * slab)
    rate = column(doppler[...].astype(jnp.float32), first_bin, bins)
    value_re, value_im = filter_taps(lag.astype(jnp.float32), beta, rate)
    for part, value in enumerate((value_re, value_im)):
        value = value.astype(jnp.bfloat16).astype(jnp.float32)
        for b in range(bins):
            rows = toeplitz_rows(value[b : b + 1, :], TILE)
            az_rows[b, part * TILE : (part + 1) * TILE, :] = rows[:, :span].astype(jnp.bfloat16)

    position = lax.broadcasted_iota(jnp.int32, (slab, extent), 1)
    bin_at = lax.broadcasted_iota(jnp.int32, (slab, extent), 0) + rg * slab
    start = column(shift[...].astype(jnp.float32), 0, slab).astype(jnp.int32)
    offset = position - bin_at - start
    mig = jnp.zeros((slab, extent), jnp.float32)
    for tap in range(weight.shape[0]):
        tap_weight = column(weight[tap : tap + 1, :].astype(jnp.float32), 0, slab)
        mig = jnp.where(offset == tap, tap_weight, mig)
    mig = mig.astype(jnp.bfloat16)

    half_len = raw.shape[2]
    early = (half_len // TILE) * TILE - extent + TILE
    near = early + extent - TILE
    far = width + extent - TILE - near

    def half(index):
        return halves[index].reshape(2 * lines, half_len)

    def add_lags(low, high):
        windows = jnp.concatenate(
            [full[:, t * TILE + low : t * TILE + high] for t in range(extent // TILE)], axis=0
        )
        return dot_nt(windows, chirp_rows[:, low:high])

    own.wait()

    @pl.when(rg == 0)
    def _():
        full[:, :near] = half(0)[:, :near]
        sums[...] = add_lags(0, early)

    @pl.when(rg == 1)
    def _():
        full[:, far:] = half(1)[:, far - half_len :]
        sums[...] = add_lags(width - early, width)

    pair.wait()

    @pl.when(rg == 0)
    def _():
        full[:, near:] = jnp.concatenate([half(0)[:, near:], half(1)], axis=1)
        sums[...] += add_lags(early, width)

    @pl.when(rg == 1)
    def _():
        full[:, :far] = jnp.concatenate([half(0), half(1)[:, : far - half_len]], axis=1)
        sums[...] += add_lags(0, width - early)

    products = sums[...]
    pieces = []
    for t in range(extent // TILE):
        product = products[2 * lines * t : 2 * lines * (t + 1)]
        real = product[:lines, :TILE] + product[lines:, TILE:]
        imag = product[lines:, :TILE] - product[:lines, TILE:]
        pieces.append(jnp.concatenate([real, imag], axis=0).astype(jnp.bfloat16))
    range_lines = jnp.concatenate(pieces, axis=1)
    moved[...] = dot_nt(mig, range_lines).astype(jnp.bfloat16).astype(jnp.float32)

    def block(index):
        return moved.at[pl.ds(pl.multiple_of(index * bins, bins), bins), :]

    copies = []
    for step in range(1, azs):
        peer = lax.rem(az + step, azs)
        copy = pltpu.make_async_remote_copy(
            src_ref=block(peer), dst_ref=slots.at[az], send_sem=turn_send.at[step],
            recv_sem=turn_recv.at[az], device_id={"az": peer}, device_id_type=MESH,
        )
        copy.start()
        copies.append(copy)
    slots[az] = block(az)[...]
    for step in range(1, azs):
        peer = lax.rem(az + step, azs)
        pltpu.make_async_remote_copy(
            src_ref=block(peer), dst_ref=slots.at[peer], send_sem=turn_send.at[step],
            recv_sem=turn_recv.at[peer], device_id={"az": peer}, device_id_type=MESH,
        ).wait_recv()

    apron = jnp.zeros((bins, (tiles_az - 1) * TILE), jnp.float32)
    for part in range(2):
        signal = jnp.concatenate(
            [slots[i][:, part * lines : (part + 1) * lines] for i in range(azs)], axis=1
        )
        signal = jnp.concatenate([apron, signal, apron], axis=1)
        for t in range(tiles_az):
            spread[part * tiles_az + t] = signal[:, t * TILE : t * TILE + span]
    for b in range(bins):
        product = dot_nt(spread[:, b, :].astype(jnp.bfloat16), az_rows[b])
        out[b, 0] = product[:tiles_az, :TILE] - product[tiles_az:, TILE:]
        out[b, 1] = product[tiles_az:, :TILE] + product[:tiles_az, TILE:]
    for copy in copies:
        copy.wait_send()


def fused(raw_echo, chirp, interp_weight, band_shift, doppler_bin):
    azs = lax.axis_size("az")
    lines, half_len = raw_echo.shape[1:]
    taps = chirp.shape[1]
    slab = interp_weight.shape[1]
    bins = slab // azs
    tiles_az = azs * lines // TILE
    span = (2 * tiles_az - 1) * TILE
    vmem = pl.BlockSpec(memory_space=pltpu.VMEM)
    result = pl.pallas_call(
        functools.partial(fused_kernel, azs),
        out_shape=jax.ShapeDtypeStruct((bins, 2, tiles_az, TILE), jnp.float32),
        in_specs=[pl.BlockSpec(memory_space=pltpu.HBM)] * 5,
        out_specs=vmem,
        scratch_shapes=[
            pltpu.VMEM(chirp.shape, chirp.dtype),
            pltpu.VMEM(interp_weight.shape, interp_weight.dtype),
            pltpu.VMEM((1, band_shift.shape[0]), band_shift.dtype),
            pltpu.VMEM((1, doppler_bin.shape[0]), doppler_bin.dtype),
            pltpu.SemaphoreType.DMA((4,)),
            pltpu.VMEM((2, 2, lines, half_len), jnp.bfloat16),
            pltpu.VMEM((2 * lines, 2 * half_len), jnp.bfloat16),
            pltpu.VMEM((2 * TILE, taps + TILE), jnp.bfloat16),
            pltpu.VMEM((bins, 2 * TILE, span), jnp.bfloat16),
            pltpu.VMEM((slab, 2 * lines), jnp.float32),
            pltpu.VMEM((azs, bins, 2 * lines), jnp.float32),
            pltpu.VMEM((2 * tiles_az, bins, span), jnp.float32),
            pltpu.VMEM(((2 * half_len - taps) // TILE * 2 * lines, 2 * TILE), jnp.float32),
            pltpu.SemaphoreType.DMA,
            pltpu.SemaphoreType.DMA,
            pltpu.SemaphoreType.DMA,
            pltpu.SemaphoreType.DMA((azs,)),
            pltpu.SemaphoreType.DMA((azs,)),
        ],
        compiler_params=pltpu.CompilerParams(
            collective_id=0, has_side_effects=True, vmem_limit_bytes=63 * 1024 * 1024
        ),
    )(raw_echo, chirp, interp_weight, band_shift.reshape(1, -1), doppler_bin.reshape(1, -1))
    return result.reshape(bins, 2, tiles_az * TILE)


def local(raw_echo, chirp, interp_weight, band_shift, doppler_bin):
    azs = lax.axis_size("az")
    lines, half_len = raw_echo.shape[1:]
    total_lines = azs * lines
    extent = 2 * half_len - chirp.shape[1]
    small = (
        lax.axis_size("rg") == 2
        and interp_weight.shape[1] == 8 * azs
        and 2 * lines == TILE
        and total_lines % TILE == 0
        and total_lines <= AZ_TAPS // 4
        and extent % TILE == 0
        and extent <= 512
    )
    run = fused if small else per_device
    return run(raw_echo, chirp, interp_weight, band_shift, doppler_bin)


def solution(mesh):
    placed = (P(None, ("scene", "az"), "rg"), P(), P(None, "rg"), P("rg"), P("scene"))
    return jax.shard_map(
        local,
        mesh=mesh,
        in_specs=placed,
        out_specs=P(("scene", "rg", "az"), None, None),
        check_vma=False,
    )
```

```python
import functools
import math

import jax
import jax.numpy as jnp
from jax import lax
from jax.experimental import pallas as pl
from jax.experimental.pallas import tpu as pltpu
from jax.sharding import PartitionSpec as P

AZ_TAPS = 2048
AZ_TILE = 128
TILE = 128
MESH = pl.DeviceIdType.MESH


def partner(value, axis, bit):
    return lax.ppermute(value, axis, [(i, i ^ 1 << bit) for i in range(lax.axis_size(axis))])


def filter_taps(offset, beta, doppler):
    centered = offset - 0.5 * AZ_TAPS
    phase = (
        math.pi * beta * (centered * centered) / AZ_TAPS
        + 2.0 * math.pi / AZ_TAPS * doppler * centered
    )
    amplitude = (0.54 - 0.46 * jnp.cos(2.0 * math.pi / (AZ_TAPS - 1) * offset)) / math.sqrt(
        0.4 * AZ_TAPS
    )
    return (amplitude * jnp.cos(phase), amplitude * jnp.sin(phase))


def shifted_rows(vector, rows):
    taps = vector.shape[0]
    padded = jnp.concatenate([vector, jnp.zeros((rows + 1,), vector.dtype)])
    repeated = jnp.tile(padded, rows)[: rows * (taps + rows)]
    return repeated.reshape(rows, taps + rows)


def range_and_migration(window, kernel, mig_matrix, tile, extent):
    lines = window.shape[1]
    width = kernel.shape[1] // 2
    count = extent // tile
    starts = jnp.arange(count, dtype=jnp.int32) * tile

    def tile_window(start):
        piece = lax.dynamic_slice_in_dim(window, start, width, 2)
        return jnp.concatenate([piece[0], piece[1]], axis=1)

    stacked = jax.vmap(tile_window)(starts).reshape(count * lines, 2 * width)
    tiles_out = lax.dot_general(
        stacked, kernel, (((1,), (1,)), ((), ())), preferred_element_type=jnp.float32
    )
    range_lines = (
        tiles_out.reshape(count, lines, 2, tile).transpose(2, 1, 0, 3).reshape(2 * lines, extent)
    )
    range_lines = range_lines.astype(jnp.bfloat16)
    moved = lax.dot_general(
        mig_matrix, range_lines, (((0,), (1,)), ((), ())), preferred_element_type=jnp.float32
    )
    return moved.astype(jnp.bfloat16).reshape(mig_matrix.shape[1], 2, lines)


def per_device(raw_echo, chirp, interp_weight, band_shift, doppler_bin):
    rg_index = lax.axis_index("rg")
    az_index = lax.axis_index("az")
    half_len = raw_echo.shape[2]
    taps = chirp.shape[1]
    bands = interp_weight.shape[0]
    slab = interp_weight.shape[1]
    extent = 2 * half_len - slab - taps
    tile = min(128, slab)
    margin_len = half_len - slab
    outgoing = lax.dynamic_slice_in_dim(raw_echo, (1 - rg_index) * slab, margin_len, 2)
    incoming = partner(outgoing, "rg", 0)
    window = jnp.where(
        rg_index == 0,
        jnp.concatenate([raw_echo, incoming], axis=2),
        jnp.concatenate([incoming, raw_echo], axis=2),
    )
    rows_re = shifted_rows(chirp[0], tile)
    rows_im = shifted_rows(chirp[1], tile)
    kernel = jnp.concatenate(
        [jnp.concatenate([rows_re, rows_im], axis=1), jnp.concatenate([-rows_im, rows_re], axis=1)],
        axis=0,
    )
    position = lax.broadcasted_iota(jnp.int32, (extent, slab), 0)
    column = lax.broadcasted_iota(jnp.int32, (extent, slab), 1)
    offset = position - column - band_shift[None, :]
    mig_matrix = jnp.zeros((extent, slab), jnp.bfloat16)
    for tap in range(bands):
        mig_matrix = mig_matrix + jnp.where(
            offset == tap, interp_weight[tap][None, :], jnp.zeros((), jnp.bfloat16)
        )
    migrated = range_and_migration(window, kernel, mig_matrix, tile, extent)
    turned = lax.all_to_all(migrated, "az", split_axis=0, concat_axis=2, tiled=True)
    bins_here = turned.shape[0]
    total_lines = turned.shape[2]
    total_bins = slab * lax.axis_size("rg")
    first_bin = rg_index * slab + az_index * bins_here
    doppler = lax.dynamic_slice_in_dim(doppler_bin, first_bin, bins_here).astype(jnp.float32)
    global_bins = (first_bin + jnp.arange(bins_here, dtype=jnp.int32)).astype(jnp.float32)
    beta = 0.5 + 0.5 * global_bins / total_bins
    span = AZ_TAPS // AZ_TILE + 1
    tile_count = total_lines // AZ_TILE
    block_count = (total_lines + AZ_TAPS) // AZ_TILE
    out_index = lax.broadcasted_iota(jnp.int32, (AZ_TILE, AZ_TILE + AZ_TAPS), 0)
    in_index = lax.broadcasted_iota(jnp.int32, (AZ_TILE, AZ_TILE + AZ_TAPS), 1)
    lag = in_index - out_index
    inside = (lag >= 0) & (lag < AZ_TAPS)
    lag_float = lag.astype(jnp.float32)

    def one_bin(args):
        signal, shift, rate = args
        padded = jnp.pad(signal, ((0, 0), (AZ_TAPS // 2, AZ_TAPS // 2)))
        blocks = padded.reshape(2, block_count, AZ_TILE)
        windows = jnp.concatenate(
            [blocks[:, start : start + tile_count] for start in range(span)], axis=2
        )
        left = jnp.concatenate([windows[0], windows[1]], axis=1)
        value_re, value_im = filter_taps(lag_float, rate, shift)
        value_re = jnp.where(inside, value_re, 0.0).astype(jnp.bfloat16)
        value_im = jnp.where(inside, value_im, 0.0).astype(jnp.bfloat16)
        az_kernel = jnp.concatenate(
            [
                jnp.concatenate([value_re, -value_im], axis=1),
                jnp.concatenate([value_im, value_re], axis=1),
            ],
            axis=0,
        )
        result = lax.dot_general(
            left, az_kernel, (((1,), (1,)), ((), ())), preferred_element_type=jnp.float32
        )
        return result.reshape(tile_count, 2, AZ_TILE).transpose(1, 0, 2).reshape(2, total_lines)

    return lax.map(one_bin, (turned, doppler, beta))


def toeplitz_rows(row, rows):
    return pltpu.roll(jnp.broadcast_to(row, (rows, row.shape[1])), 0, 1, stride=1, stride_axis=0)


def column(row, first, rows):
    width = row.shape[1]
    lane = lax.broadcasted_iota(jnp.int32, (rows, width), 1)
    sub = lax.broadcasted_iota(jnp.int32, (rows, width), 0)
    picked = jnp.where(lane == sub + first, jnp.broadcast_to(row, (rows, width)), 0.0)
    return jnp.sum(picked, axis=1, keepdims=True)


def dot_nt(left, right):
    return lax.dot_general(
        left, right, (((1,), (1,)), ((), ())), preferred_element_type=jnp.float32
    )


def fused_kernel(
    azs, raw, chirp_in, weight_in, shift_in, doppler_in, out,
    chirp, weight, shift, doppler, small_sem, halves, full, chirp_rows, az_rows, moved, slots, spread, sums,
    local_sem, pair_send, pair_recv, turn_send, turn_recv,
):
    az = lax.axis_index("az")
    rg = lax.axis_index("rg")
    lines = raw.shape[1]
    slab = weight_in.shape[1]
    bins = out.shape[0]
    tiles_az = out.shape[2]
    taps = chirp.shape[1]
    width = taps + TILE
    extent = full.shape[1] - taps

    barrier = pltpu.get_barrier_semaphore()
    pl.semaphore_signal(barrier, inc=1, device_id={"rg": 1 - rg}, device_id_type=MESH)
    for step in range(1, azs):
        pl.semaphore_signal(
            barrier, inc=1, device_id={"az": lax.rem(az + step, azs)}, device_id_type=MESH
        )
    loads = [
        pltpu.make_async_copy(source, target, small_sem.at[i])
        for i, (source, target) in enumerate(
            ((chirp_in, chirp), (doppler_in, doppler), (shift_in, shift), (weight_in, weight))
        )
    ]
    for load in loads:
        load.start()
    own = pltpu.make_async_copy(raw, halves.at[rg], local_sem)
    own.start()
    pl.semaphore_wait(barrier, azs)
    pair = pltpu.make_async_remote_copy(
        src_ref=raw, dst_ref=halves.at[rg], send_sem=pair_send, recv_sem=pair_recv,
        device_id={"rg": 1 - rg}, device_id_type=MESH,
    )
    pair.start()

    for load in loads:
        load.wait()

    for part in range(2):
        padded = jnp.concatenate(
            [chirp[part : part + 1, :].astype(jnp.float32), jnp.zeros((1, TILE), jnp.float32)],
            axis=1,
        )
        chirp_rows[part * TILE : (part + 1) * TILE, :] = toeplitz_rows(padded, TILE).astype(
            jnp.bfloat16
        )

    position = lax.broadcasted_iota(jnp.int32, (slab, extent), 1)
    bin_at = lax.broadcasted_iota(jnp.int32, (slab, extent), 0) + rg * slab
    start = column(shift[...].astype(jnp.float32), 0, slab).astype(jnp.int32)
    offset = position - bin_at - start
    mig = jnp.zeros((slab, extent), jnp.float32)
    for tap in range(weight.shape[0]):
        tap_weight = column(weight[tap : tap + 1, :].astype(jnp.float32), 0, slab)
        mig = jnp.where(offset == tap, tap_weight, mig)
    mig = mig.astype(jnp.bfloat16)

    half_len = raw.shape[2]
    early = (half_len // TILE) * TILE - extent + TILE
    near = early + extent - TILE
    far = width + extent - TILE - near

    def half(index):
        return halves[index].reshape(2 * lines, half_len)

    def add_lags(low, high):
        windows = jnp.concatenate(
            [full[:, t * TILE + low : t * TILE + high] for t in range(extent // TILE)], axis=0
        )
        return dot_nt(windows, chirp_rows[:, low:high])

    own.wait()

    @pl.when(rg == 0)
    def _():
        full[:, :near] = half(0)[:, :near]
        sums[...] = add_lags(0, early)

    @pl.when(rg == 1)
    def _():
        full[:, far:] = half(1)[:, far - half_len :]
        sums[...] = add_lags(width - early, width)

    pair.wait()

    @pl.when(rg == 0)
    def _():
        full[:, near:] = jnp.concatenate([half(0)[:, near:], half(1)], axis=1)
        sums[...] += add_lags(early, width)

    @pl.when(rg == 1)
    def _():
        full[:, :far] = jnp.concatenate([half(0), half(1)[:, : far - half_len]], axis=1)
        sums[...] += add_lags(0, width - early)

    products = sums[...]
    pieces = []
    for t in range(extent // TILE):
        product = products[2 * lines * t : 2 * lines * (t + 1)]
        real = product[:lines, :TILE] + product[lines:, TILE:]
        imag = product[lines:, :TILE] - product[:lines, TILE:]
        pieces.append(jnp.concatenate([real, imag], axis=0).astype(jnp.bfloat16))
    range_lines = jnp.concatenate(pieces, axis=1)
    moved[...] = dot_nt(mig, range_lines).astype(jnp.bfloat16).astype(jnp.float32)

    def block(index):
        return moved.at[pl.ds(pl.multiple_of(index * bins, bins), bins), :]

    copies = []
    for step in range(1, azs):
        peer = lax.rem(az + step, azs)
        copy = pltpu.make_async_remote_copy(
            src_ref=block(peer), dst_ref=slots.at[az], send_sem=turn_send.at[step],
            recv_sem=turn_recv.at[az], device_id={"az": peer}, device_id_type=MESH,
        )
        copy.start()
        copies.append(copy)
    slots[az] = block(az)[...]

    span = (2 * tiles_az - 1) * TILE
    wheel = span + TILE
    first_bin = rg * slab + az * bins
    place = lax.broadcasted_iota(jnp.int32, (bins, wheel), 1)
    lag = place + AZ_TAPS // 2 - (tiles_az - 1) * TILE - jnp.where(place >= span, wheel, 0)
    bin_index = first_bin + lax.broadcasted_iota(jnp.int32, (bins, wheel), 0)
    beta = 0.5 + 0.5 * bin_index.astype(jnp.float32) / (2 * slab)
    rate = column(doppler[...].astype(jnp.float32), first_bin, bins)
    value_re, value_im = filter_taps(lag.astype(jnp.float32), beta, rate)
    for part, value in enumerate((value_re, value_im)):
        value = value.astype(jnp.bfloat16).astype(jnp.float32)
        for b in range(bins):
            rows = toeplitz_rows(value[b : b + 1, :], TILE)
            az_rows[b, part * TILE : (part + 1) * TILE, :] = rows[:, :span].astype(jnp.bfloat16)

    for step in range(1, azs):
        peer = lax.rem(az + step, azs)
        pltpu.make_async_remote_copy(
            src_ref=block(peer), dst_ref=slots.at[peer], send_sem=turn_send.at[step],
            recv_sem=turn_recv.at[peer], device_id={"az": peer}, device_id_type=MESH,
        ).wait_recv()

    apron = jnp.zeros((bins, (tiles_az - 1) * TILE), jnp.float32)
    for part in range(2):
        signal = jnp.concatenate(
            [slots[i][:, part * lines : (part + 1) * lines] for i in range(azs)], axis=1
        )
        signal = jnp.concatenate([apron, signal, apron], axis=1)
        for t in range(tiles_az):
            spread[part * tiles_az + t] = signal[:, t * TILE : t * TILE + span]
    for b in range(bins):
        product = dot_nt(spread[:, b, :].astype(jnp.bfloat16), az_rows[b])
        out[b, 0] = product[:tiles_az, :TILE] - product[tiles_az:, TILE:]
        out[b, 1] = product[tiles_az:, :TILE] + product[:tiles_az, TILE:]
    for copy in copies:
        copy.wait_send()


def fused(raw_echo, chirp, interp_weight, band_shift, doppler_bin):
    azs = lax.axis_size("az")
    lines, half_len = raw_echo.shape[1:]
    taps = chirp.shape[1]
    slab = interp_weight.shape[1]
    bins = slab // azs
    tiles_az = azs * lines // TILE
    span = (2 * tiles_az - 1) * TILE
    vmem = pl.BlockSpec(memory_space=pltpu.VMEM)
    result = pl.pallas_call(
        functools.partial(fused_kernel, azs),
        out_shape=jax.ShapeDtypeStruct((bins, 2, tiles_az, TILE), jnp.float32),
        in_specs=[pl.BlockSpec(memory_space=pltpu.HBM)] * 5,
        out_specs=vmem,
        scratch_shapes=[
            pltpu.VMEM(chirp.shape, chirp.dtype),
            pltpu.VMEM(interp_weight.shape, interp_weight.dtype),
            pltpu.VMEM((1, band_shift.shape[0]), band_shift.dtype),
            pltpu.VMEM((1, doppler_bin.shape[0]), doppler_bin.dtype),
            pltpu.SemaphoreType.DMA((4,)),
            pltpu.VMEM((2, 2, lines, half_len), jnp.bfloat16),
            pltpu.VMEM((2 * lines, 2 * half_len), jnp.bfloat16),
            pltpu.VMEM((2 * TILE, taps + TILE), jnp.bfloat16),
            pltpu.VMEM((bins, 2 * TILE, span), jnp.bfloat16),
            pltpu.VMEM((slab, 2 * lines), jnp.float32),
            pltpu.VMEM((azs, bins, 2 * lines), jnp.float32),
            pltpu.VMEM((2 * tiles_az, bins, span), jnp.float32),
            pltpu.VMEM(((2 * half_len - taps) // TILE * 2 * lines, 2 * TILE), jnp.float32),
            pltpu.SemaphoreType.DMA,
            pltpu.SemaphoreType.DMA,
            pltpu.SemaphoreType.DMA,
            pltpu.SemaphoreType.DMA((azs,)),
            pltpu.SemaphoreType.DMA((azs,)),
        ],
        compiler_params=pltpu.CompilerParams(
            collective_id=0, has_side_effects=True, vmem_limit_bytes=63 * 1024 * 1024
        ),
    )(raw_echo, chirp, interp_weight, band_shift.reshape(1, -1), doppler_bin.reshape(1, -1))
    return result.reshape(bins, 2, tiles_az * TILE)


def local(raw_echo, chirp, interp_weight, band_shift, doppler_bin):
    azs = lax.axis_size("az")
    lines, half_len = raw_echo.shape[1:]
    total_lines = azs * lines
    extent = 2 * half_len - chirp.shape[1]
    small = (
        lax.axis_size("rg") == 2
        and interp_weight.shape[1] == 8 * azs
        and 2 * lines == TILE
        and total_lines % TILE == 0
        and total_lines <= AZ_TAPS // 4
        and extent % TILE == 0
        and extent <= 512
    )
    run = fused if small else per_device
    return run(raw_echo, chirp, interp_weight, band_shift, doppler_bin)


def solution(mesh):
    placed = (P(None, ("scene", "az"), "rg"), P(), P(None, "rg"), P("rg"), P("scene"))
    return jax.shard_map(
        local,
        mesh=mesh,
        in_specs=placed,
        out_specs=P(("scene", "rg", "az"), None, None),
        check_vma=False,
    )
```

```python
import functools
import math

import jax
import jax.numpy as jnp
from jax import lax
from jax.experimental import pallas as pl
from jax.experimental.pallas import tpu as pltpu
from jax.sharding import PartitionSpec as P

AZ_TAPS = 2048
AZ_TILE = 128
TILE = 128
MESH = pl.DeviceIdType.MESH


def partner(value, axis, bit):
    return lax.ppermute(value, axis, [(i, i ^ 1 << bit) for i in range(lax.axis_size(axis))])


def filter_taps(offset, beta, doppler):
    centered = offset - 0.5 * AZ_TAPS
    phase = (
        math.pi * beta * (centered * centered) / AZ_TAPS
        + 2.0 * math.pi / AZ_TAPS * doppler * centered
    )
    amplitude = (0.54 - 0.46 * jnp.cos(2.0 * math.pi / (AZ_TAPS - 1) * offset)) / math.sqrt(
        0.4 * AZ_TAPS
    )
    return (amplitude * jnp.cos(phase), amplitude * jnp.sin(phase))


def shifted_rows(vector, rows):
    taps = vector.shape[0]
    padded = jnp.concatenate([vector, jnp.zeros((rows + 1,), vector.dtype)])
    repeated = jnp.tile(padded, rows)[: rows * (taps + rows)]
    return repeated.reshape(rows, taps + rows)


def range_and_migration(window, kernel, mig_matrix, tile, extent):
    lines = window.shape[1]
    width = kernel.shape[1] // 2
    count = extent // tile
    starts = jnp.arange(count, dtype=jnp.int32) * tile

    def tile_window(start):
        piece = lax.dynamic_slice_in_dim(window, start, width, 2)
        return jnp.concatenate([piece[0], piece[1]], axis=1)

    stacked = jax.vmap(tile_window)(starts).reshape(count * lines, 2 * width)
    tiles_out = lax.dot_general(
        stacked, kernel, (((1,), (1,)), ((), ())), preferred_element_type=jnp.float32
    )
    range_lines = (
        tiles_out.reshape(count, lines, 2, tile).transpose(2, 1, 0, 3).reshape(2 * lines, extent)
    )
    range_lines = range_lines.astype(jnp.bfloat16)
    moved = lax.dot_general(
        mig_matrix, range_lines, (((0,), (1,)), ((), ())), preferred_element_type=jnp.float32
    )
    return moved.astype(jnp.bfloat16).reshape(mig_matrix.shape[1], 2, lines)


def per_device(raw_echo, chirp, interp_weight, band_shift, doppler_bin):
    rg_index = lax.axis_index("rg")
    az_index = lax.axis_index("az")
    half_len = raw_echo.shape[2]
    taps = chirp.shape[1]
    bands = interp_weight.shape[0]
    slab = interp_weight.shape[1]
    extent = 2 * half_len - slab - taps
    tile = min(128, slab)
    margin_len = half_len - slab
    outgoing = lax.dynamic_slice_in_dim(raw_echo, (1 - rg_index) * slab, margin_len, 2)
    incoming = partner(outgoing, "rg", 0)
    window = jnp.where(
        rg_index == 0,
        jnp.concatenate([raw_echo, incoming], axis=2),
        jnp.concatenate([incoming, raw_echo], axis=2),
    )
    rows_re = shifted_rows(chirp[0], tile)
    rows_im = shifted_rows(chirp[1], tile)
    kernel = jnp.concatenate(
        [jnp.concatenate([rows_re, rows_im], axis=1), jnp.concatenate([-rows_im, rows_re], axis=1)],
        axis=0,
    )
    position = lax.broadcasted_iota(jnp.int32, (extent, slab), 0)
    column = lax.broadcasted_iota(jnp.int32, (extent, slab), 1)
    offset = position - column - band_shift[None, :]
    mig_matrix = jnp.zeros((extent, slab), jnp.bfloat16)
    for tap in range(bands):
        mig_matrix = mig_matrix + jnp.where(
            offset == tap, interp_weight[tap][None, :], jnp.zeros((), jnp.bfloat16)
        )
    migrated = range_and_migration(window, kernel, mig_matrix, tile, extent)
    turned = lax.all_to_all(migrated, "az", split_axis=0, concat_axis=2, tiled=True)
    bins_here = turned.shape[0]
    total_lines = turned.shape[2]
    total_bins = slab * lax.axis_size("rg")
    first_bin = rg_index * slab + az_index * bins_here
    doppler = lax.dynamic_slice_in_dim(doppler_bin, first_bin, bins_here).astype(jnp.float32)
    global_bins = (first_bin + jnp.arange(bins_here, dtype=jnp.int32)).astype(jnp.float32)
    beta = 0.5 + 0.5 * global_bins / total_bins
    span = AZ_TAPS // AZ_TILE + 1
    tile_count = total_lines // AZ_TILE
    block_count = (total_lines + AZ_TAPS) // AZ_TILE
    out_index = lax.broadcasted_iota(jnp.int32, (AZ_TILE, AZ_TILE + AZ_TAPS), 0)
    in_index = lax.broadcasted_iota(jnp.int32, (AZ_TILE, AZ_TILE + AZ_TAPS), 1)
    lag = in_index - out_index
    inside = (lag >= 0) & (lag < AZ_TAPS)
    lag_float = lag.astype(jnp.float32)

    def one_bin(args):
        signal, shift, rate = args
        padded = jnp.pad(signal, ((0, 0), (AZ_TAPS // 2, AZ_TAPS // 2)))
        blocks = padded.reshape(2, block_count, AZ_TILE)
        windows = jnp.concatenate(
            [blocks[:, start : start + tile_count] for start in range(span)], axis=2
        )
        left = jnp.concatenate([windows[0], windows[1]], axis=1)
        value_re, value_im = filter_taps(lag_float, rate, shift)
        value_re = jnp.where(inside, value_re, 0.0).astype(jnp.bfloat16)
        value_im = jnp.where(inside, value_im, 0.0).astype(jnp.bfloat16)
        az_kernel = jnp.concatenate(
            [
                jnp.concatenate([value_re, -value_im], axis=1),
                jnp.concatenate([value_im, value_re], axis=1),
            ],
            axis=0,
        )
        result = lax.dot_general(
            left, az_kernel, (((1,), (1,)), ((), ())), preferred_element_type=jnp.float32
        )
        return result.reshape(tile_count, 2, AZ_TILE).transpose(1, 0, 2).reshape(2, total_lines)

    return lax.map(one_bin, (turned, doppler, beta))


def toeplitz_rows(row, rows):
    return pltpu.roll(jnp.broadcast_to(row, (rows, row.shape[1])), 0, 1, stride=1, stride_axis=0)


def column(row, first, rows):
    width = row.shape[1]
    lane = lax.broadcasted_iota(jnp.int32, (rows, width), 1)
    sub = lax.broadcasted_iota(jnp.int32, (rows, width), 0)
    picked = jnp.where(lane == sub + first, jnp.broadcast_to(row, (rows, width)), 0.0)
    return jnp.sum(picked, axis=1, keepdims=True)


def dot_nt(left, right):
    return lax.dot_general(
        left, right, (((1,), (1,)), ((), ())), preferred_element_type=jnp.float32
    )


def fused_kernel(
    azs, raw, chirp_in, weight_in, shift_in, doppler_in, out,
    chirp, weight, shift, doppler, small_sem, halves, full, chirp_rows, az_rows, moved, slots, spread, sums,
    local_sem, pair_send, pair_recv, turn_send, turn_recv,
):
    az = lax.axis_index("az")
    rg = lax.axis_index("rg")
    lines = raw.shape[1]
    slab = weight_in.shape[1]
    bins = out.shape[0]
    tiles_az = out.shape[2]
    taps = chirp.shape[1]
    width = taps + TILE
    extent = full.shape[1] - taps

    barrier = pltpu.get_barrier_semaphore()
    pl.semaphore_signal(barrier, inc=1, device_id={"rg": 1 - rg}, device_id_type=MESH)
    for step in range(1, azs):
        pl.semaphore_signal(
            barrier, inc=1, device_id={"az": lax.rem(az + step, azs)}, device_id_type=MESH
        )
    loads = [
        pltpu.make_async_copy(source, target, small_sem.at[i])
        for i, (source, target) in enumerate(
            ((chirp_in, chirp), (doppler_in, doppler), (shift_in, shift), (weight_in, weight))
        )
    ]
    for load in loads:
        load.start()
    own = pltpu.make_async_copy(raw, halves.at[rg], local_sem)
    own.start()
    pl.semaphore_wait(barrier, azs)
    pair = pltpu.make_async_remote_copy(
        src_ref=raw, dst_ref=halves.at[rg], send_sem=pair_send, recv_sem=pair_recv,
        device_id={"rg": 1 - rg}, device_id_type=MESH,
    )
    pair.start()

    for load in loads:
        load.wait()

    for part in range(2):
        padded = jnp.concatenate(
            [chirp[part : part + 1, :].astype(jnp.float32), jnp.zeros((1, TILE), jnp.float32)],
            axis=1,
        )
        chirp_rows[part * TILE : (part + 1) * TILE, :] = toeplitz_rows(padded, TILE).astype(
            jnp.bfloat16
        )

    position = lax.broadcasted_iota(jnp.int32, (slab, extent), 1)
    bin_at = lax.broadcasted_iota(jnp.int32, (slab, extent), 0) + rg * slab
    start = column(shift[...].astype(jnp.float32), 0, slab).astype(jnp.int32)
    offset = position - bin_at - start
    mig = jnp.zeros((slab, extent), jnp.float32)
    for tap in range(weight.shape[0]):
        tap_weight = column(weight[tap : tap + 1, :].astype(jnp.float32), 0, slab)
        mig = jnp.where(offset == tap, tap_weight, mig)
    mig = mig.astype(jnp.bfloat16)

    half_len = raw.shape[2]
    early = (half_len // TILE) * TILE - extent + TILE
    near = early + extent - TILE
    far = width + extent - TILE - near

    def half(index):
        return halves[index].reshape(2 * lines, half_len)

    def add_lags(low, high):
        windows = jnp.concatenate(
            [full[:, t * TILE + low : t * TILE + high] for t in range(extent // TILE)], axis=0
        )
        return dot_nt(windows, chirp_rows[:, low:high])

    own.wait()

    @pl.when(rg == 0)
    def _():
        full[:, :near] = half(0)[:, :near]
        sums[...] = add_lags(0, early)

    @pl.when(rg == 1)
    def _():
        full[:, far:] = half(1)[:, far - half_len :]
        sums[...] = add_lags(width - early, width)

    pair.wait()

    @pl.when(rg == 0)
    def _():
        full[:, near:] = jnp.concatenate([half(0)[:, near:], half(1)], axis=1)
        sums[...] += add_lags(early, width)

    @pl.when(rg == 1)
    def _():
        full[:, :far] = jnp.concatenate([half(0), half(1)[:, : far - half_len]], axis=1)
        sums[...] += add_lags(0, width - early)

    products = sums[...]
    pieces = []
    for t in range(extent // TILE):
        product = products[2 * lines * t : 2 * lines * (t + 1)]
        real = product[:lines, :TILE] + product[lines:, TILE:]
        imag = product[lines:, :TILE] - product[:lines, TILE:]
        pieces.append(jnp.concatenate([real, imag], axis=0).astype(jnp.bfloat16))
    range_lines = jnp.concatenate(pieces, axis=1)
    moved[...] = dot_nt(mig, range_lines).astype(jnp.bfloat16).astype(jnp.float32)

    def block(index):
        return moved.at[pl.ds(pl.multiple_of(index * bins, bins), bins), :]

    copies = []
    for step in range(1, azs):
        peer = lax.rem(az + step, azs)
        copy = pltpu.make_async_remote_copy(
            src_ref=block(peer), dst_ref=slots.at[az], send_sem=turn_send.at[step],
            recv_sem=turn_recv.at[az], device_id={"az": peer}, device_id_type=MESH,
        )
        copy.start()
        copies.append(copy)
    slots[az] = block(az)[...]

    span = (2 * tiles_az - 1) * TILE
    wheel = 2 * TILE
    first_bin = rg * slab + az * bins
    ring = (2 * tiles_az - 1) * wheel
    place = lax.broadcasted_iota(jnp.int32, (bins, ring), 1)
    inner = lax.rem(place, wheel)
    back = inner - jnp.where(inner < TILE, 0, wheel)
    lag = place // wheel * TILE + AZ_TAPS // 2 - (tiles_az - 1) * TILE - back
    bin_index = first_bin + lax.broadcasted_iota(jnp.int32, (bins, ring), 0)
    beta = 0.5 + 0.5 * bin_index.astype(jnp.float32) / (2 * slab)
    rate = column(doppler[...].astype(jnp.float32), first_bin, bins)
    value_re, value_im = filter_taps(lag.astype(jnp.float32), beta, rate)
    for part, value in enumerate((value_re, value_im)):
        value = value.astype(jnp.bfloat16).astype(jnp.float32)
        for b in range(bins):
            for d in range(2 * tiles_az - 1):
                rows = toeplitz_rows(value[b : b + 1, d * wheel : (d + 1) * wheel], TILE)
                az_rows[b, d * TILE : (d + 1) * TILE, part * TILE : (part + 1) * TILE] = rows[
                    :, :TILE
                ].astype(jnp.bfloat16)

    for step in range(1, azs):
        peer = lax.rem(az + step, azs)
        pltpu.make_async_remote_copy(
            src_ref=block(peer), dst_ref=slots.at[peer], send_sem=turn_send.at[step],
            recv_sem=turn_recv.at[peer], device_id={"az": peer}, device_id_type=MESH,
        ).wait_recv()

    apron = jnp.zeros((bins, (tiles_az - 1) * TILE), jnp.float32)
    for part in range(2):
        signal = jnp.concatenate(
            [slots[i][:, part * lines : (part + 1) * lines] for i in range(azs)], axis=1
        )
        signal = jnp.concatenate([apron, signal, apron], axis=1)
        for t in range(tiles_az):
            spread[part * tiles_az + t] = signal[:, t * TILE : t * TILE + span]
    for b in range(bins):
        product = jnp.dot(
            spread[:, b, :].astype(jnp.bfloat16), az_rows[b], preferred_element_type=jnp.float32
        )
        out[b, 0] = product[:tiles_az, :TILE] - product[tiles_az:, TILE:]
        out[b, 1] = product[tiles_az:, :TILE] + product[:tiles_az, TILE:]
    for copy in copies:
        copy.wait_send()


def fused(raw_echo, chirp, interp_weight, band_shift, doppler_bin):
    azs = lax.axis_size("az")
    lines, half_len = raw_echo.shape[1:]
    taps = chirp.shape[1]
    slab = interp_weight.shape[1]
    bins = slab // azs
    tiles_az = azs * lines // TILE
    span = (2 * tiles_az - 1) * TILE
    vmem = pl.BlockSpec(memory_space=pltpu.VMEM)
    result = pl.pallas_call(
        functools.partial(fused_kernel, azs),
        out_shape=jax.ShapeDtypeStruct((bins, 2, tiles_az, TILE), jnp.float32),
        in_specs=[pl.BlockSpec(memory_space=pltpu.HBM)] * 5,
        out_specs=vmem,
        scratch_shapes=[
            pltpu.VMEM(chirp.shape, chirp.dtype),
            pltpu.VMEM(interp_weight.shape, interp_weight.dtype),
            pltpu.VMEM((1, band_shift.shape[0]), band_shift.dtype),
            pltpu.VMEM((1, doppler_bin.shape[0]), doppler_bin.dtype),
            pltpu.SemaphoreType.DMA((4,)),
            pltpu.VMEM((2, 2, lines, half_len), jnp.bfloat16),
            pltpu.VMEM((2 * lines, 2 * half_len), jnp.bfloat16),
            pltpu.VMEM((2 * TILE, taps + TILE), jnp.bfloat16),
            pltpu.VMEM((bins, span, 2 * TILE), jnp.bfloat16),
            pltpu.VMEM((slab, 2 * lines), jnp.float32),
            pltpu.VMEM((azs, bins, 2 * lines), jnp.float32),
            pltpu.VMEM((2 * tiles_az, bins, span), jnp.float32),
            pltpu.VMEM(((2 * half_len - taps) // TILE * 2 * lines, 2 * TILE), jnp.float32),
            pltpu.SemaphoreType.DMA,
            pltpu.SemaphoreType.DMA,
            pltpu.SemaphoreType.DMA,
            pltpu.SemaphoreType.DMA((azs,)),
            pltpu.SemaphoreType.DMA((azs,)),
        ],
        compiler_params=pltpu.CompilerParams(
            collective_id=0, has_side_effects=True, vmem_limit_bytes=63 * 1024 * 1024
        ),
    )(raw_echo, chirp, interp_weight, band_shift.reshape(1, -1), doppler_bin.reshape(1, -1))
    return result.reshape(bins, 2, tiles_az * TILE)


def local(raw_echo, chirp, interp_weight, band_shift, doppler_bin):
    azs = lax.axis_size("az")
    lines, half_len = raw_echo.shape[1:]
    total_lines = azs * lines
    extent = 2 * half_len - chirp.shape[1]
    small = (
        lax.axis_size("rg") == 2
        and interp_weight.shape[1] == 8 * azs
        and 2 * lines == TILE
        and total_lines % TILE == 0
        and total_lines <= AZ_TAPS // 4
        and extent % TILE == 0
        and extent <= 512
    )
    run = fused if small else per_device
    return run(raw_echo, chirp, interp_weight, band_shift, doppler_bin)


def solution(mesh):
    placed = (P(None, ("scene", "az"), "rg"), P(), P(None, "rg"), P("rg"), P("scene"))
    return jax.shard_map(
        local,
        mesh=mesh,
        in_specs=placed,
        out_specs=P(("scene", "rg", "az"), None, None),
        check_vma=False,
    )
```

```python
import functools
import math

import jax
import jax.numpy as jnp
from jax import lax
from jax.experimental import pallas as pl
from jax.experimental.pallas import tpu as pltpu
from jax.sharding import PartitionSpec as P

AZ_TAPS = 2048
AZ_TILE = 128
TILE = 128
MESH = pl.DeviceIdType.MESH


def partner(value, axis, bit):
    return lax.ppermute(value, axis, [(i, i ^ 1 << bit) for i in range(lax.axis_size(axis))])


def filter_taps(offset, beta, doppler):
    centered = offset - 0.5 * AZ_TAPS
    phase = (
        math.pi * beta * (centered * centered) / AZ_TAPS
        + 2.0 * math.pi / AZ_TAPS * doppler * centered
    )
    amplitude = (0.54 - 0.46 * jnp.cos(2.0 * math.pi / (AZ_TAPS - 1) * offset)) / math.sqrt(
        0.4 * AZ_TAPS
    )
    return (amplitude * jnp.cos(phase), amplitude * jnp.sin(phase))


def shifted_rows(vector, rows):
    taps = vector.shape[0]
    padded = jnp.concatenate([vector, jnp.zeros((rows + 1,), vector.dtype)])
    repeated = jnp.tile(padded, rows)[: rows * (taps + rows)]
    return repeated.reshape(rows, taps + rows)


def range_and_migration(window, kernel, mig_matrix, tile, extent):
    lines = window.shape[1]
    width = kernel.shape[1] // 2
    count = extent // tile
    starts = jnp.arange(count, dtype=jnp.int32) * tile

    def tile_window(start):
        piece = lax.dynamic_slice_in_dim(window, start, width, 2)
        return jnp.concatenate([piece[0], piece[1]], axis=1)

    stacked = jax.vmap(tile_window)(starts).reshape(count * lines, 2 * width)
    tiles_out = lax.dot_general(
        stacked, kernel, (((1,), (1,)), ((), ())), preferred_element_type=jnp.float32
    )
    range_lines = (
        tiles_out.reshape(count, lines, 2, tile).transpose(2, 1, 0, 3).reshape(2 * lines, extent)
    )
    range_lines = range_lines.astype(jnp.bfloat16)
    moved = lax.dot_general(
        mig_matrix, range_lines, (((0,), (1,)), ((), ())), preferred_element_type=jnp.float32
    )
    return moved.astype(jnp.bfloat16).reshape(mig_matrix.shape[1], 2, lines)


def per_device(raw_echo, chirp, interp_weight, band_shift, doppler_bin):
    rg_index = lax.axis_index("rg")
    az_index = lax.axis_index("az")
    half_len = raw_echo.shape[2]
    taps = chirp.shape[1]
    bands = interp_weight.shape[0]
    slab = interp_weight.shape[1]
    extent = 2 * half_len - slab - taps
    tile = min(128, slab)
    margin_len = half_len - slab
    outgoing = lax.dynamic_slice_in_dim(raw_echo, (1 - rg_index) * slab, margin_len, 2)
    incoming = partner(outgoing, "rg", 0)
    window = jnp.where(
        rg_index == 0,
        jnp.concatenate([raw_echo, incoming], axis=2),
        jnp.concatenate([incoming, raw_echo], axis=2),
    )
    rows_re = shifted_rows(chirp[0], tile)
    rows_im = shifted_rows(chirp[1], tile)
    kernel = jnp.concatenate(
        [jnp.concatenate([rows_re, rows_im], axis=1), jnp.concatenate([-rows_im, rows_re], axis=1)],
        axis=0,
    )
    position = lax.broadcasted_iota(jnp.int32, (extent, slab), 0)
    column = lax.broadcasted_iota(jnp.int32, (extent, slab), 1)
    offset = position - column - band_shift[None, :]
    mig_matrix = jnp.zeros((extent, slab), jnp.bfloat16)
    for tap in range(bands):
        mig_matrix = mig_matrix + jnp.where(
            offset == tap, interp_weight[tap][None, :], jnp.zeros((), jnp.bfloat16)
        )
    migrated = range_and_migration(window, kernel, mig_matrix, tile, extent)
    turned = lax.all_to_all(migrated, "az", split_axis=0, concat_axis=2, tiled=True)
    bins_here = turned.shape[0]
    total_lines = turned.shape[2]
    total_bins = slab * lax.axis_size("rg")
    first_bin = rg_index * slab + az_index * bins_here
    doppler = lax.dynamic_slice_in_dim(doppler_bin, first_bin, bins_here).astype(jnp.float32)
    global_bins = (first_bin + jnp.arange(bins_here, dtype=jnp.int32)).astype(jnp.float32)
    beta = 0.5 + 0.5 * global_bins / total_bins
    span = AZ_TAPS // AZ_TILE + 1
    tile_count = total_lines // AZ_TILE
    block_count = (total_lines + AZ_TAPS) // AZ_TILE
    out_index = lax.broadcasted_iota(jnp.int32, (AZ_TILE, AZ_TILE + AZ_TAPS), 0)
    in_index = lax.broadcasted_iota(jnp.int32, (AZ_TILE, AZ_TILE + AZ_TAPS), 1)
    lag = in_index - out_index
    inside = (lag >= 0) & (lag < AZ_TAPS)
    lag_float = lag.astype(jnp.float32)

    def one_bin(args):
        signal, shift, rate = args
        padded = jnp.pad(signal, ((0, 0), (AZ_TAPS // 2, AZ_TAPS // 2)))
        blocks = padded.reshape(2, block_count, AZ_TILE)
        windows = jnp.concatenate(
            [blocks[:, start : start + tile_count] for start in range(span)], axis=2
        )
        left = jnp.concatenate([windows[0], windows[1]], axis=1)
        value_re, value_im = filter_taps(lag_float, rate, shift)
        value_re = jnp.where(inside, value_re, 0.0).astype(jnp.bfloat16)
        value_im = jnp.where(inside, value_im, 0.0).astype(jnp.bfloat16)
        az_kernel = jnp.concatenate(
            [
                jnp.concatenate([value_re, -value_im], axis=1),
                jnp.concatenate([value_im, value_re], axis=1),
            ],
            axis=0,
        )
        result = lax.dot_general(
            left, az_kernel, (((1,), (1,)), ((), ())), preferred_element_type=jnp.float32
        )
        return result.reshape(tile_count, 2, AZ_TILE).transpose(1, 0, 2).reshape(2, total_lines)

    return lax.map(one_bin, (turned, doppler, beta))


def toeplitz_rows(row, rows):
    return pltpu.roll(jnp.broadcast_to(row, (rows, row.shape[1])), 0, 1, stride=1, stride_axis=0)


def column(row, first, rows):
    width = row.shape[1]
    lane = lax.broadcasted_iota(jnp.int32, (rows, width), 1)
    sub = lax.broadcasted_iota(jnp.int32, (rows, width), 0)
    picked = jnp.where(lane == sub + first, jnp.broadcast_to(row, (rows, width)), 0.0)
    return jnp.sum(picked, axis=1, keepdims=True)


def dot_nt(left, right):
    return lax.dot_general(
        left, right, (((1,), (1,)), ((), ())), preferred_element_type=jnp.float32
    )


def fused_kernel(
    azs, raw, chirp_in, weight_in, shift_in, doppler_in, out,
    chirp, weight, shift, doppler, small_sem, halves, full, chirp_rows, az_rows, moved, slots, spread, sums,
    local_sem, pair_send, pair_recv, turn_send, turn_recv,
):
    az = lax.axis_index("az")
    rg = lax.axis_index("rg")
    lines = raw.shape[1]
    slab = weight_in.shape[1]
    bins = out.shape[0]
    tiles_az = out.shape[2]
    taps = chirp.shape[1]
    width = taps + TILE
    extent = full.shape[1] - taps

    barrier = pltpu.get_barrier_semaphore()
    pl.semaphore_signal(barrier, inc=1, device_id={"rg": 1 - rg}, device_id_type=MESH)
    for step in range(1, azs):
        pl.semaphore_signal(
            barrier, inc=1, device_id={"az": lax.rem(az + step, azs)}, device_id_type=MESH
        )
    loads = [
        pltpu.make_async_copy(source, target, small_sem.at[i])
        for i, (source, target) in enumerate(
            ((chirp_in, chirp), (doppler_in, doppler), (shift_in, shift), (weight_in, weight))
        )
    ]
    for load in loads:
        load.start()
    own = pltpu.make_async_copy(raw, halves.at[rg], local_sem)
    own.start()
    pl.semaphore_wait(barrier, azs)
    pair = pltpu.make_async_remote_copy(
        src_ref=raw, dst_ref=halves.at[rg], send_sem=pair_send, recv_sem=pair_recv,
        device_id={"rg": 1 - rg}, device_id_type=MESH,
    )
    pair.start()

    for load in loads:
        load.wait()

    for part in range(2):
        padded = jnp.concatenate(
            [chirp[part : part + 1, :].astype(jnp.float32), jnp.zeros((1, TILE), jnp.float32)],
            axis=1,
        )
        chirp_rows[part * TILE : (part + 1) * TILE, :] = toeplitz_rows(padded, TILE).astype(
            jnp.bfloat16
        )

    span = (2 * tiles_az - 1) * TILE
    wheel = 2 * TILE
    first_bin = rg * slab + az * bins
    ring = (2 * tiles_az - 1) * wheel
    place = lax.broadcasted_iota(jnp.int32, (bins, ring), 1)
    inner = lax.rem(place, wheel)
    back = inner - jnp.where(inner < TILE, 0, wheel)
    lag = place // wheel * TILE + AZ_TAPS // 2 - (tiles_az - 1) * TILE - back
    bin_index = first_bin + lax.broadcasted_iota(jnp.int32, (bins, ring), 0)
    beta = 0.5 + 0.5 * bin_index.astype(jnp.float32) / (2 * slab)
    rate = column(doppler[...].astype(jnp.float32), first_bin, bins)
    value_re, value_im = filter_taps(lag.astype(jnp.float32), beta, rate)

    position = lax.broadcasted_iota(jnp.int32, (slab, extent), 1)
    bin_at = lax.broadcasted_iota(jnp.int32, (slab, extent), 0) + rg * slab
    start = column(shift[...].astype(jnp.float32), 0, slab).astype(jnp.int32)
    offset = position - bin_at - start
    mig = jnp.zeros((slab, extent), jnp.float32)
    for tap in range(weight.shape[0]):
        tap_weight = column(weight[tap : tap + 1, :].astype(jnp.float32), 0, slab)
        mig = jnp.where(offset == tap, tap_weight, mig)
    mig = mig.astype(jnp.bfloat16)

    half_len = raw.shape[2]
    early = (half_len // TILE) * TILE - extent + TILE
    near = early + extent - TILE
    far = width + extent - TILE - near

    def half(index):
        return halves[index].reshape(2 * lines, half_len)

    def add_lags(low, high):
        windows = jnp.concatenate(
            [full[:, t * TILE + low : t * TILE + high] for t in range(extent // TILE)], axis=0
        )
        return dot_nt(windows, chirp_rows[:, low:high])

    own.wait()

    @pl.when(rg == 0)
    def _():
        full[:, :near] = half(0)[:, :near]
        sums[...] = add_lags(0, early)

    @pl.when(rg == 1)
    def _():
        full[:, far:] = half(1)[:, far - half_len :]
        sums[...] = add_lags(width - early, width)

    pair.wait()

    @pl.when(rg == 0)
    def _():
        full[:, near:] = jnp.concatenate([half(0)[:, near:], half(1)], axis=1)
        sums[...] += add_lags(early, width)

    @pl.when(rg == 1)
    def _():
        full[:, :far] = jnp.concatenate([half(0), half(1)[:, : far - half_len]], axis=1)
        sums[...] += add_lags(0, width - early)

    products = sums[...]
    pieces = []
    for t in range(extent // TILE):
        product = products[2 * lines * t : 2 * lines * (t + 1)]
        real = product[:lines, :TILE] + product[lines:, TILE:]
        imag = product[lines:, :TILE] - product[:lines, TILE:]
        pieces.append(jnp.concatenate([real, imag], axis=0).astype(jnp.bfloat16))
    range_lines = jnp.concatenate(pieces, axis=1)
    moved[...] = dot_nt(mig, range_lines).astype(jnp.bfloat16).astype(jnp.float32)

    def block(index):
        return moved.at[pl.ds(pl.multiple_of(index * bins, bins), bins), :]

    copies = []
    for step in range(1, azs):
        peer = lax.rem(az + step, azs)
        copy = pltpu.make_async_remote_copy(
            src_ref=block(peer), dst_ref=slots.at[az], send_sem=turn_send.at[step],
            recv_sem=turn_recv.at[az], device_id={"az": peer}, device_id_type=MESH,
        )
        copy.start()
        copies.append(copy)
    slots[az] = block(az)[...]

    for part, value in enumerate((value_re, value_im)):
        value = value.astype(jnp.bfloat16).astype(jnp.float32)
        for b in range(bins):
            for d in range(2 * tiles_az - 1):
                rows = toeplitz_rows(value[b : b + 1, d * wheel : (d + 1) * wheel], TILE)
                az_rows[b, d * TILE : (d + 1) * TILE, part * TILE : (part + 1) * TILE] = rows[
                    :, :TILE
                ].astype(jnp.bfloat16)

    for step in range(1, azs):
        peer = lax.rem(az + step, azs)
        pltpu.make_async_remote_copy(
            src_ref=block(peer), dst_ref=slots.at[peer], send_sem=turn_send.at[step],
            recv_sem=turn_recv.at[peer], device_id={"az": peer}, device_id_type=MESH,
        ).wait_recv()

    apron = jnp.zeros((bins, (tiles_az - 1) * TILE), jnp.float32)
    for part in range(2):
        signal = jnp.concatenate(
            [slots[i][:, part * lines : (part + 1) * lines] for i in range(azs)], axis=1
        )
        signal = jnp.concatenate([apron, signal, apron], axis=1)
        for t in range(tiles_az):
            spread[part * tiles_az + t] = signal[:, t * TILE : t * TILE + span]
    for b in range(bins):
        product = jnp.dot(
            spread[:, b, :].astype(jnp.bfloat16), az_rows[b], preferred_element_type=jnp.float32
        )
        out[b, 0] = product[:tiles_az, :TILE] - product[tiles_az:, TILE:]
        out[b, 1] = product[tiles_az:, :TILE] + product[:tiles_az, TILE:]
    for copy in copies:
        copy.wait_send()


def fused(raw_echo, chirp, interp_weight, band_shift, doppler_bin):
    azs = lax.axis_size("az")
    lines, half_len = raw_echo.shape[1:]
    taps = chirp.shape[1]
    slab = interp_weight.shape[1]
    bins = slab // azs
    tiles_az = azs * lines // TILE
    span = (2 * tiles_az - 1) * TILE
    vmem = pl.BlockSpec(memory_space=pltpu.VMEM)
    result = pl.pallas_call(
        functools.partial(fused_kernel, azs),
        out_shape=jax.ShapeDtypeStruct((bins, 2, tiles_az, TILE), jnp.float32),
        in_specs=[pl.BlockSpec(memory_space=pltpu.HBM)] * 5,
        out_specs=vmem,
        scratch_shapes=[
            pltpu.VMEM(chirp.shape, chirp.dtype),
            pltpu.VMEM(interp_weight.shape, interp_weight.dtype),
            pltpu.VMEM((1, band_shift.shape[0]), band_shift.dtype),
            pltpu.VMEM((1, doppler_bin.shape[0]), doppler_bin.dtype),
            pltpu.SemaphoreType.DMA((4,)),
            pltpu.VMEM((2, 2, lines, half_len), jnp.bfloat16),
            pltpu.VMEM((2 * lines, 2 * half_len), jnp.bfloat16),
            pltpu.VMEM((2 * TILE, taps + TILE), jnp.bfloat16),
            pltpu.VMEM((bins, span, 2 * TILE), jnp.bfloat16),
            pltpu.VMEM((slab, 2 * lines), jnp.float32),
            pltpu.VMEM((azs, bins, 2 * lines), jnp.float32),
            pltpu.VMEM((2 * tiles_az, bins, span), jnp.float32),
            pltpu.VMEM(((2 * half_len - taps) // TILE * 2 * lines, 2 * TILE), jnp.float32),
            pltpu.SemaphoreType.DMA,
            pltpu.SemaphoreType.DMA,
            pltpu.SemaphoreType.DMA,
            pltpu.SemaphoreType.DMA((azs,)),
            pltpu.SemaphoreType.DMA((azs,)),
        ],
        compiler_params=pltpu.CompilerParams(
            collective_id=0, has_side_effects=True, vmem_limit_bytes=63 * 1024 * 1024
        ),
    )(raw_echo, chirp, interp_weight, band_shift.reshape(1, -1), doppler_bin.reshape(1, -1))
    return result.reshape(bins, 2, tiles_az * TILE)


def local(raw_echo, chirp, interp_weight, band_shift, doppler_bin):
    azs = lax.axis_size("az")
    lines, half_len = raw_echo.shape[1:]
    total_lines = azs * lines
    extent = 2 * half_len - chirp.shape[1]
    small = (
        lax.axis_size("rg") == 2
        and interp_weight.shape[1] == 8 * azs
        and 2 * lines == TILE
        and total_lines % TILE == 0
        and total_lines <= AZ_TAPS // 4
        and extent % TILE == 0
        and extent <= 512
    )
    run = fused if small else per_device
    return run(raw_echo, chirp, interp_weight, band_shift, doppler_bin)


def solution(mesh):
    placed = (P(None, ("scene", "az"), "rg"), P(), P(None, "rg"), P("rg"), P("scene"))
    return jax.shard_map(
        local,
        mesh=mesh,
        in_specs=placed,
        out_specs=P(("scene", "rg", "az"), None, None),
        check_vma=False,
    )
```
